1024 devices in a mesh: own: 64 (over z, x), rep: 16 (over y, core).
Axes of the slice: x: 8, y: 8, z: 8, core: 2. Of those that a mesh axis runs over, the one named last changes fastest.
Arguments:
- features: bfloat16 [4096, 128, 512], P(('own', 'rep')), may hold values from -6 to 6
- adj_cols: int32 [4096, 4], P(('own', 'rep')), may hold values from 0 to 4095, as said below
- adj_counts: int32 [4096], P(('own', 'rep')), may hold values from 2 to 4, as said below
- adj_vals: bfloat16 [4096, 4, 128, 128], P(('own', 'rep')), may hold values from -0.3125 to 0.3125
- weight: bfloat16 [512, 512], replicated, may hold values from -0.25 to 0.25
- cotangent: bfloat16 [4096, 128, 512], P(('own', 'rep')), may hold values from -6 to 6
Outputs:
- output: bfloat16 [4096, 128, 512], P(('own', 'rep'))
- grad_features: float32 [4096, 128, 512], P(('own', 'rep'))
- grad_weight: float32 [512, 512], replicated
The draws below stay inside these ranges and needn't reach their ends.
Inputs may be any that keep to these rules, and one draw needn't show every extreme that they name: `adj_cols`: the block columns of a row's slots are distinct and lie within 2 blocks of the row, counted cyclically over the 4096 blocks; slot 0 names the row itself, slot 1 the block before it for even rows and the block after it for odd rows. `adj_counts`: loads differ between devices; 4 is reached in every draw.
All inputs are finite; a program needn't handle non-finite values.
Results may differ from the reference program's by a relative error of at most 0.0054.
Values may be sent and summed in bfloat16 or wider, within the bound.
A program may use at most 32 MiB of HBM per device.

```python
import jax
import jax.numpy as jnp
from jax import lax

F = 512
BLK = 128
KMAX = 4
REACH = 2
NBO = 4
NB = 4096
NODES = 524288


def draw_adj_counts(key, part):
    key = jax.random.fold_in(key, 11)
    key_heavy, key_raw, key_spot = jax.random.split(key, 3)
    devices = NB // NBO
    heaviness = jax.random.randint(key_heavy, (devices, 1), 0, KMAX - 1)
    raw_counts = jax.random.randint(key_raw, (devices, NBO), 0, 2 ** 20)
    counts = (2 + jnp.remainder(raw_counts, heaviness + 1)).reshape(-1)
    spot = jax.random.randint(key_spot, (), 0, NB)
    counts = counts.at[spot].set(KMAX)
    return counts.astype(jnp.int32)


def draw_adj_cols(key, part):
    key = jax.random.fold_in(key, 23)
    span = 2 * REACH + 1
    rows = jnp.arange(NB, dtype=jnp.int32)
    offset_values = jnp.arange(span, dtype=jnp.int32) - REACH
    beside = jnp.where(rows % 2 == 0, -1, 1).astype(jnp.int32)
    taken = (offset_values[None, :] == 0) | (offset_values[None, :] == beside[:, None])
    scores = jax.random.randint(key, (NB, span), 0, 2 ** 20) * span + jnp.arange(span, dtype=jnp.int32)[None, :]
    scores = jnp.where(taken, scores + 2 ** 26, scores)
    order = jnp.argsort(scores, axis=1)
    table = jnp.broadcast_to(offset_values[None, :], (NB, span))
    remaining_parts = jnp.take_along_axis(table, order[:, :KMAX - 2], axis=1)
    offsets = jnp.concatenate([jnp.zeros((NB, 1), jnp.int32), beside[:, None], remaining_parts], axis=1)
    return jnp.remainder(rows[:, None] + offsets, NB).astype(jnp.int32)


def level_of(own_key, dims, cuts, smallest, top_value):
    loudness = 1.0
    for position, parts in cuts:
        heights = jax.random.uniform(jax.random.fold_in(jax.random.fold_in(own_key, 6), position), (parts,), jnp.float32, smallest / len(cuts), top_value / len(cuts))
        loudness = loudness * jnp.repeat(jnp.exp(heights), dims[position] // parts).reshape((-1,) + (1,) * (len(dims) - 1 - position))
    return loudness


def noise(own_key, extent, spread, reach, pieces=(), held_as=jnp.bfloat16):
    factor_of = level_of(own_key, extent, pieces, -0.22, 0.18) if pieces else 1.0
    values = jax.random.normal(own_key, extent, jnp.float32) * spread * factor_of
    return jnp.minimum(jnp.maximum(values, -reach), reach).astype(held_as)


def setup_inputs(seed: int = 0) -> dict:
    key_list = jax.random.split(jax.random.key(seed), 7)
    return {
        "features": noise(key_list[0], (NB, BLK, F), 1.0, 6.0, ((0, 1024),)),
        "adj_cols": draw_adj_cols(jax.random.fold_in(key_list[6], 71), 0),
        "adj_counts": draw_adj_counts(jax.random.fold_in(key_list[6], 71), 0),
        "adj_vals": noise(key_list[3], (NB, KMAX, BLK, BLK), (BLK * 3) ** -0.5, 0.3125, ((0, 1024),)),
        "weight": noise(key_list[4], (F, F), F ** -0.5, 0.25),
        "cotangent": noise(key_list[5], (NB, BLK, F), 1.0, 6.0, ((0, 1024),)),
    }


def reference(features, adj_cols, adj_counts, adj_vals, weight, cotangent):
    slot_ids = jnp.arange(KMAX, dtype=jnp.int32)
    used = slot_ids[None, :] < adj_counts[:, None]

    def row_block(row):
        values = jnp.where(used[row][:, None, None], adj_vals[row], jnp.zeros((), adj_vals.dtype)).astype(jnp.float32)
        blocks = features[adj_cols[row]].astype(jnp.float32)
        return jnp.einsum("kab,kbf->af", values, blocks)

    row_ids = jnp.arange(NB, dtype=jnp.int32)
    summed = lax.map(row_block, row_ids)
    hidden = summed.astype(jnp.bfloat16).reshape(NODES, F)
    preact = jnp.dot(hidden, weight, preferred_element_type=jnp.float32)
    output = jax.nn.silu(preact).astype(jnp.bfloat16).reshape(NB, BLK, F)
    sigmoid_pre = jax.nn.sigmoid(preact)
    slope = sigmoid_pre * (1.0 + preact * (1.0 - sigmoid_pre))
    grad_pre = (cotangent.reshape(NODES, F).astype(jnp.float32) * slope).astype(jnp.bfloat16)
    grad_hidden = jnp.dot(grad_pre, weight.T, preferred_element_type=jnp.float32).astype(jnp.bfloat16).reshape(NB, BLK, F)
    grad_weight = jnp.dot(hidden.T, grad_pre, preferred_element_type=jnp.float32)
    offset_values = jnp.arange(2 * REACH + 1, dtype=jnp.int32) - REACH

    def column_block(column):
        rows = jnp.remainder(column - offset_values, NB).astype(jnp.int32)
        hits = (adj_cols[rows] == column) & used[rows]
        values = adj_vals[rows].astype(jnp.float32)
        combined = jnp.sum(jnp.where(hits[:, :, None, None], values, jnp.zeros((), jnp.float32)), axis=1)
        grads = grad_hidden[rows].astype(jnp.float32)
        return jnp.einsum("oab,oaf->bf", combined, grads)

    grad_features = lax.map(column_block, row_ids)
    return output, grad_features, grad_weight
```

```python
import functools

import jax
import jax.numpy as jnp
from jax import lax
from jax.experimental import pallas as pl
from jax.experimental.pallas import tpu as pltpu
from jax.sharding import PartitionSpec as P

MESH = pl.DeviceIdType.MESH
F32 = jnp.float32
BF16 = jnp.bfloat16
REACH = 2
BLK = 128
PIECES = 2
ORDERS = ((2, 1, 0), (1, 0, 2), (0, 2, 1))


def dot(a, b, dims=((1,), (0,))):
    return lax.dot_general(a, b, (dims, ((), ())), preferred_element_type=F32)


def main_kernel(
    n, total_blocks,
    cols_h, counts_h, feat, vals, wgt, cot,
    out, gf, fa, fb, fc,
    cols, counts, ext, vals_v, w_v, cot_v, band, hid, grad_pre, hid_t, acc, own_half,
    core_out, core_in, rim_out, rim_in,
    sa, sb, sc, ra, rb, rc, ta, tb, tc, ua, ub, uc,
    load_sem, halo_send, halo_recv, rim_send, rim_recv, core_send, core_recv,
    step_send, step_recv, gather_send, gather_recv, fwd_send, fwd_recv,
):
    own = lax.axis_index("own")
    rep = lax.axis_index("rep")
    core = rep % 2
    place = (own // n, own % n, rep // 2)
    me = own * (2 * n) + rep
    count = n * n * n * 2

    def device(z, x, y, c):
        return {"own": z * n + x, "rep": y * 2 + c}

    def peer(axis, value):
        p = list(place)
        p[axis] = value
        return device(*p, core)

    def at_index(i):
        return {"own": i // (2 * n), "rep": i % (2 * n)}

    right = at_index((me + 1) % count)
    left = at_index((me + count - 1) % count)
    partner = device(*place, 1 - core)
    hops = sorted(range(1, n), key=lambda d: -min(d, n - d))

    loads = [
        pltpu.make_async_copy(feat, ext.at[pl.ds(256, 512)], load_sem.at[0]),
        pltpu.make_async_copy(vals, vals_v, load_sem.at[1]),
        pltpu.make_async_copy(wgt, w_v, load_sem.at[2]),
        pltpu.make_async_copy(cot, cot_v, load_sem.at[3]),
        pltpu.make_async_copy(cols_h, cols, load_sem.at[4]),
        pltpu.make_async_copy(counts_h, counts, load_sem.at[5]),
    ]
    for copy in loads:
        copy.start()

    barrier = pltpu.get_barrier_semaphore()
    for axis in range(3):
        for d in hops:
            pl.semaphore_signal(
                barrier, inc=1, device_id=peer(axis, (place[axis] + d) % n), device_id_type=MESH
            )
    pl.semaphore_signal(barrier, inc=1, device_id=left, device_id_type=MESH)
    pl.semaphore_signal(barrier, inc=1, device_id=right, device_id_type=MESH)

    row0 = me * 4
    loads[4].wait()
    loads[5].wait()
    loads[1].wait()
    for r in range(4):
        h, q = divmod(r, 2)
        rows = slice(q * BLK, (q + 1) * BLK)
        beside = -1 if q == 0 else 1
        third = counts[r] > 2
        fourth = counts[r] > 3
        c2, c3 = cols[r, 2], cols[r, 3]
        v2, v3 = vals_v[r * 4 + 2], vals_v[r * 4 + 3]
        for e in range(6):
            o = e - q - REACH
            if o == 0:
                block = vals_v[r * 4]
            elif o == beside:
                block = vals_v[r * 4 + 1]
            elif -REACH <= o <= REACH:
                name = (row0 + r + o + total_blocks) % total_blocks
                use2 = jnp.logical_and(third, c2 == name).astype(F32).astype(BF16)
                use3 = jnp.logical_and(fourth, c3 == name).astype(F32).astype(BF16)
                block = v2 * use2 + v3 * use3
            else:
                block = jnp.zeros((BLK, BLK), BF16)
            band[h, rows, e * BLK : (e + 1) * BLK] = block

    loads[0].wait()
    hid[0:256, :] = dot(band[0, :, 256:768], ext[256:768, :])
    hid[256:512, :] = dot(band[1, :, 0:512], ext[256:768, :])

    pl.semaphore_wait(barrier, 3 * (n - 1) + 2)

    send_right = pltpu.make_async_remote_copy(
        src_ref=ext.at[pl.ds(512, 256)], dst_ref=ext.at[pl.ds(0, 256)],
        send_sem=halo_send.at[0], recv_sem=halo_recv.at[0],
        device_id=right, device_id_type=MESH,
    )
    send_left = pltpu.make_async_remote_copy(
        src_ref=ext.at[pl.ds(256, 256)], dst_ref=ext.at[pl.ds(768, 256)],
        send_sem=halo_send.at[1], recv_sem=halo_recv.at[1],
        device_id=left, device_id_type=MESH,
    )
    send_right.start()
    send_left.start()
    loads[2].wait()
    loads[3].wait()

    def forward(h):
        rows = pl.ds(pl.multiple_of(256 * h, 256), 256)
        rim_cols = pl.ds(pl.multiple_of(512 * h, 512), 256)
        halo_rows = pl.ds(pl.multiple_of(768 * h, 256), 256)
        hidden = (hid[rows, :] + dot(band[h, :, rim_cols], ext[halo_rows, :])).astype(BF16)
        hid_t[...] = hidden.T
        preact = dot(hidden, w_v[...])
        sig = 1.0 / (1.0 + jnp.exp(-preact))
        out[rows, :] = (preact * sig).astype(BF16)
        slope = sig * (1.0 + preact * (1.0 - sig))
        grad_pre[rows, :] = (cot_v[rows, :].astype(F32) * slope).astype(BF16)

    def rim(h):
        return pltpu.make_async_remote_copy(
            src_ref=rim_out.at[h], dst_ref=rim_in.at[1 - h],
            send_sem=rim_send.at[h], recv_sem=rim_recv.at[1 - h],
            device_id=at_index((me + count - 1 + 2 * h) % count), device_id_type=MESH,
        )

    def backward(h, first):
        rows = pl.ds(pl.multiple_of(256 * h, 256), 256)
        rim_cols = pl.ds(pl.multiple_of(512 * h, 512), 256)
        inner_cols = pl.ds(pl.multiple_of(256 * (1 - h), 256), 512)
        grad_hidden = dot(grad_pre[rows, :], w_v[...], ((1,), (1,))).astype(BF16)
        rim_out[h] = dot(band[h, :, rim_cols], grad_hidden, ((0,), (0,))).astype(BF16)
        rim(h).start()
        inner = dot(band[h, :, inner_cols], grad_hidden, ((0,), (0,)))
        if first:
            gf[...] = inner
        else:
            gf[...] += inner

    near, far = 1 - core, core
    pltpu.make_async_remote_copy(
        src_ref=ext.at[pl.ds(256, 256)], dst_ref=ext.at[pl.ds(pl.multiple_of(768 * near, 256), 256)],
        send_sem=halo_send.at[0], recv_sem=halo_recv.at[near],
        device_id=partner, device_id_type=MESH,
    ).wait_recv()
    forward(near)
    acc[...] = dot(hid_t[...], grad_pre[pl.ds(pl.multiple_of(256 * near, 256), 256), :])
    backward(near, True)
    pltpu.make_async_remote_copy(
        src_ref=ext.at[pl.ds(256, 256)], dst_ref=ext.at[pl.ds(pl.multiple_of(768 * far, 256), 256)],
        send_sem=halo_send.at[0], recv_sem=halo_recv.at[far],
        device_id=partner, device_id_type=MESH,
    ).wait_recv()
    forward(far)

    far_rows = pl.ds(pl.multiple_of(256 * far, 256), 256)
    size = 256 // PIECES
    core_copies = []
    for q in range(PIECES):
        here = pl.ds(pl.multiple_of(256 * (1 - core) + size * q, size), size)
        core_out[q] = (acc[here, :] + dot(hid_t[here, :], grad_pre[far_rows, :])).astype(BF16)
        copy = pltpu.make_async_remote_copy(
            src_ref=core_out.at[q], dst_ref=core_in.at[q],
            send_sem=core_send.at[q], recv_sem=core_recv.at[q],
            device_id=partner, device_id_type=MESH,
        )
        copy.start()
        core_copies.append(copy)
    mine = pl.ds(pl.multiple_of(256 * core, 256), 256)
    own_half[...] = acc[mine, :] + dot(hid_t[mine, :], grad_pre[far_rows, :])

    width = 256 // n
    low = width // 2
    for q in range(PIECES):
        core_copies[q].wait_recv()
        chip = (own_half[size * q : size * (q + 1), :] + core_in[q].astype(F32)).astype(BF16)
        for i in range(n // PIECES):
            k = q * (n // PIECES) + i
            sa[k] = chip[width * i : width * i + low, 0:384]
            sb[k] = chip[width * i + low : width * (i + 1), 0:384]
            sc[k] = chip[width * i : width * (i + 1), 384:512]

    parts = ((sa, ra, ta, ua, fa), (sb, rb, tb, ub, fb), (sc, rc, tc, uc, fc))

    def send(src, dst, part, step, axis, value):
        pltpu.make_async_remote_copy(
            src_ref=src, dst_ref=dst, send_sem=step_send.at[part, step], recv_sem=step_recv.at[part, step],
            device_id=peer(axis, value), device_id_type=MESH,
        ).start()

    def arrived(buf, part, step):
        whole = buf.at[pl.ds(0, n - 1)]
        pltpu.make_async_remote_copy(
            src_ref=whole, dst_ref=whole, send_sem=step_send.at[part, step], recv_sem=step_recv.at[part, step],
            device_id=partner, device_id_type=MESH,
        ).wait_recv()

    def summed(buf):
        total = buf[0].astype(F32)
        for i in range(1, n):
            total = total + buf[i].astype(F32)
        return total.astype(BF16)

    for d in hops:
        for p, (s, r, t, u, f) in enumerate(parts):
            axis = ORDERS[p][0]
            j = (place[axis] + d) % n
            send(s.at[j], r.at[place[axis]], p, 0, axis, j)
    for p, (s, r, t, u, f) in enumerate(parts):
        i = place[ORDERS[p][0]]
        r[i] = s[i]
    backward(far, False)

    for step in (1, 2):
        for p, part in enumerate(parts):
            axis = ORDERS[p][step]
            arrived(part[step], p, step - 1)
            part[step + 1][place[axis]] = summed(part[step])
        for d in hops:
            for p, part in enumerate(parts):
                axis = ORDERS[p][step]
                here = part[step + 1].at[place[axis]]
                send(here, here, p, step, axis, (place[axis] + d) % n)
        if step == 2:
            for h in range(2):
                pltpu.make_async_remote_copy(
                    src_ref=rim_out.at[h], dst_ref=rim_in.at[h],
                    send_sem=rim_send.at[h], recv_sem=rim_recv.at[h],
                    device_id=partner, device_id_type=MESH,
                ).wait_recv()
                gf[256 * h : 256 * (h + 1), :] += rim_in[h].astype(F32)

    for p, (s, r, t, u, f) in enumerate(parts):
        arrived(u, p, 2)
        f[core, place[ORDERS[p][0]]] = summed(u)

    def gather(p, f, target, slot):
        here = f.at[core, slot]
        axis = ORDERS[p][0]
        return pltpu.make_async_remote_copy(
            src_ref=here, dst_ref=here, send_sem=gather_send.at[p], recv_sem=gather_recv.at[p, slot],
            device_id=peer(axis, target), device_id_type=MESH,
        )

    def onward(p, f, slot):
        here = f.at[core, slot]
        return pltpu.make_async_remote_copy(
            src_ref=here, dst_ref=here, send_sem=fwd_send.at[p], recv_sem=fwd_recv.at[p],
            device_id=partner, device_id_type=MESH,
        )

    for d in hops:
        for p, part in enumerate(parts):
            i = place[ORDERS[p][0]]
            gather(p, part[4], (i + d) % n, i).start()
    for p, part in enumerate(parts):
        onward(p, part[4], place[ORDERS[p][0]]).start()
    for d in hops[::-1]:
        for p, part in enumerate(parts):
            i = place[ORDERS[p][0]]
            j = (i + d) % n
            gather(p, part[4], j, j).wait_recv()
            onward(p, part[4], j).start()

    send_right.wait_send()
    send_left.wait_send()
    for h in range(2):
        pltpu.make_async_remote_copy(
            src_ref=rim_out.at[h], dst_ref=rim_in.at[h],
            send_sem=rim_send.at[h], recv_sem=rim_recv.at[h],
            device_id=partner, device_id_type=MESH,
        ).wait_send()
    for copy in core_copies:
        copy.wait_send()
    for p, part in enumerate(parts):
        for step in range(3):
            whole = part[0].at[pl.ds(0, n - 1)]
            pltpu.make_async_remote_copy(
                src_ref=whole, dst_ref=whole, send_sem=step_send.at[p, step], recv_sem=step_recv.at[p, step],
                device_id=partner, device_id_type=MESH,
            ).wait_send()
        whole = part[4].at[core, pl.ds(0, n - 1)]
        pltpu.make_async_remote_copy(
            src_ref=whole, dst_ref=whole, send_sem=gather_send.at[p], recv_sem=fwd_recv.at[p],
            device_id=partner, device_id_type=MESH,
        ).wait_send()
        for_partner = part[4].at[core]
        from_partner = part[4].at[1 - core]
        pltpu.make_async_remote_copy(
            src_ref=for_partner, dst_ref=from_partner, send_sem=fwd_send.at[p], recv_sem=fwd_recv.at[p],
            device_id=partner, device_id_type=MESH,
        ).wait()


def write_kernel(n, out, gf, fa, fb, fc, out_r, gf_r, gw_r, gw, sems):
    copies = [
        pltpu.make_async_copy(out, out_r, sems.at[0]),
        pltpu.make_async_copy(gf, gf_r, sems.at[1]),
    ]
    for copy in copies:
        copy.start()
    width = 256 // n
    low = width // 2
    for c in range(2):
        for k in range(n):
            top = 256 * c + width * k
            gw[top : top + low, 0:384] = fa[c, k].astype(F32)
            gw[top + low : top + width, 0:384] = fb[c, k].astype(F32)
            gw[top : top + width, 384:512] = fc[c, k].astype(F32)
        rows = pl.ds(256 * c, 256)
        copy = pltpu.make_async_copy(gw.at[rows], gw_r.at[rows], sems.at[2 + c])
        copy.start()
        copies.append(copy)
    for copy in copies:
        copy.wait()


def per_device(n, features, adj_cols, adj_counts, adj_vals, weight, cotangent):
    width = 256 // n
    low = width // 2
    vmem = pl.BlockSpec(memory_space=pltpu.VMEM)
    smem = pl.BlockSpec(memory_space=pltpu.SMEM)
    anyw = pl.BlockSpec(memory_space=pl.ANY)
    hbm = pl.BlockSpec(memory_space=pltpu.HBM)
    shapes = ((n, low, 384), (n, low, 384), (n, width, 128))
    dma = pltpu.SemaphoreType.DMA
    steps = [pltpu.VMEM(s, BF16) for _ in range(4) for s in shapes]
    args = (
        adj_cols,
        adj_counts,
        features.reshape(512, 512),
        adj_vals.reshape(16, BLK, BLK),
        weight,
        cotangent.reshape(512, 512),
    )
    out, gf, fa, fb, fc = pl.pallas_call(
        functools.partial(main_kernel, n, 4 * 2 * n**3),
        out_shape=(
            pltpu.VMEM((512, 512), BF16),
            pltpu.VMEM((512, 512), F32),
            *[pltpu.VMEM((2,) + s, BF16) for s in shapes],
        ),
        in_specs=[hbm] * 6,
        out_specs=(vmem,) * 5,
        scratch_shapes=[
            pltpu.SMEM((4, 4), jnp.int32),
            pltpu.SMEM((4,), jnp.int32),
            pltpu.VMEM((1024, 512), BF16),
            pltpu.VMEM((16, BLK, BLK), BF16),
            pltpu.VMEM((512, 512), BF16),
            pltpu.VMEM((512, 512), BF16),
            pltpu.VMEM((2, 256, 768), BF16),
            pltpu.VMEM((512, 512), F32),
            pltpu.VMEM((512, 512), BF16),
            pltpu.VMEM((512, 256), BF16),
            pltpu.VMEM((512, 512), F32),
            pltpu.VMEM((256, 512), F32),
            pltpu.VMEM((PIECES, 256 // PIECES, 512), BF16),
            pltpu.VMEM((PIECES, 256 // PIECES, 512), BF16),
            pltpu.VMEM((2, 256, 512), BF16),
            pltpu.VMEM((2, 256, 512), BF16),
            *steps,
            dma((6,)), dma((2,)), dma((2,)), dma((2,)), dma((2,)), dma((PIECES,)), dma((PIECES,)),
            dma((3, 3)), dma((3, 3)), dma((3,)), dma((3, n)), dma((3,)), dma((3,)),
        ],
        compiler_params=pltpu.CompilerParams(
            collective_id=0, has_side_effects=True, vmem_limit_bytes=40 * 2**20
        ),
        name="layer",
    )(*[pltpu.with_memory_space_constraint(a, pltpu.HBM) for a in args])
    out, gf, gw = pl.pallas_call(
        functools.partial(write_kernel, n),
        out_shape=(
            jax.ShapeDtypeStruct((512, 512), BF16),
            jax.ShapeDtypeStruct((512, 512), F32),
            jax.ShapeDtypeStruct((512, 512), F32),
        ),
        in_specs=[vmem] * 5,
        out_specs=(anyw,) * 3,
        scratch_shapes=[pltpu.VMEM((512, 512), F32), dma((4,))],
        compiler_params=pltpu.CompilerParams(vmem_limit_bytes=16 * 2**20),
        name="write",
    )(out, gf, fa, fb, fc)
    return out.reshape(4, BLK, 512), gf.reshape(4, BLK, 512), gw


def solution(mesh):
    n = mesh.shape["rep"] // 2
    both = ("own", "rep")
    return jax.shard_map(
        functools.partial(per_device, n),
        mesh=mesh,
        in_specs=(
            P(both, None, None),
            P(both, None),
            P(both),
            P(both, None, None, None),
            P(),
            P(both, None, None),
        ),
        out_specs=(P(both, None, None), P(both, None, None), P()),
        check_vma=False,
    )
```

```python
import functools

import jax
import jax.numpy as jnp
from jax import lax
from jax.experimental import pallas as pl
from jax.experimental.pallas import tpu as pltpu
from jax.sharding import PartitionSpec as P

MESH = pl.DeviceIdType.MESH
F32 = jnp.float32
BF16 = jnp.bfloat16
REACH = 2
BLK = 128
PIECES = 2
FAR = 3
ORDERS = ((1, 0, 2), (0, 2, 1), (2, 1, 0))


def dot(a, b, dims=((1,), (0,))):
    return lax.dot_general(a, b, (dims, ((), ())), preferred_element_type=F32)


def main_kernel(
    n, total_blocks,
    cols_h, counts_h, feat, vals, wgt, cot,
    out, gf, fa, fb, fc,
    cols, counts, ext, vals_v, w_v, cot_v, band, hid, grad_hid, grad_pre, hid_t, acc, own_half,
    core_out, core_in, rim_out, rim_in,
    sa, sb, sc, ra, rb, rc, ta, tb, tc, ua, ub, uc,
    ready, load_sem, halo_send, halo_recv, rim_send, rim_recv, core_send, core_recv,
    step_send, step_recv, gather_send, gather_recv, fwd_send, fwd_recv,
):
    own = lax.axis_index("own")
    rep = lax.axis_index("rep")
    core = rep % 2
    place = (own // n, own % n, rep // 2)
    me = own * (2 * n) + rep
    count = n * n * n * 2

    def device(z, x, y, c):
        return {"own": z * n + x, "rep": y * 2 + c}

    def peer(axis, value):
        p = list(place)
        p[axis] = value
        return device(*p, core)

    def at_index(i):
        return {"own": i // (2 * n), "rep": i % (2 * n)}

    right = at_index((me + 1) % count)
    left = at_index((me + count - 1) % count)
    partner = device(*place, 1 - core)
    hops = sorted(range(1, n), key=lambda d: -min(d, n - d))

    loads = [
        pltpu.make_async_copy(feat, ext.at[pl.ds(256, 512)], load_sem.at[0]),
        pltpu.make_async_copy(vals, vals_v, load_sem.at[1]),
        pltpu.make_async_copy(wgt, w_v, load_sem.at[2]),
        pltpu.make_async_copy(cot, cot_v, load_sem.at[3]),
        pltpu.make_async_copy(cols_h, cols, load_sem.at[4]),
        pltpu.make_async_copy(counts_h, counts, load_sem.at[5]),
    ]
    barrier = pltpu.get_barrier_semaphore()
    for neighbour in (left, right):
        pl.semaphore_signal(barrier, inc=1, device_id=neighbour, device_id_type=MESH)
    for copy in loads:
        copy.start()
    beside = [
        (axis, d) for d in sorted({d for d in (1, 2, n - 2, n - 1) if 0 < d < n}) for axis in range(3)
    ]
    for axis, d in beside:
        pl.semaphore_signal(
            barrier, inc=1, device_id=peer(axis, (place[axis] + d) % n), device_id_type=MESH
        )

    loads[0].wait()
    pl.semaphore_wait(barrier, len(beside) + 2)
    def halo(h):
        return pltpu.make_async_remote_copy(
            src_ref=ext.at[pl.ds(pl.multiple_of(256 + 256 * h, 256), 256)],
            dst_ref=ext.at[pl.ds(pl.multiple_of(768 * (1 - h), 256), 256)],
            send_sem=halo_send.at[h], recv_sem=halo_recv.at[1 - h],
            device_id=at_index((me + count - 1 + 2 * h) % count), device_id_type=MESH,
        )

    near, far = 1 - core, core
    halo(far).start()
    halo(near).start()
    for axis, d in beside:
        pl.semaphore_signal(
            ready, inc=1, device_id=peer(axis, (place[axis] + d) % n), device_id_type=MESH
        )

    row0 = me * 4
    loads[4].wait()
    loads[5].wait()
    loads[1].wait()
    for r in range(4):
        h, q = divmod(r, 2)
        rows = slice(q * BLK, (q + 1) * BLK)
        by = -1 if q == 0 else 1
        third = counts[r] > 2
        fourth = counts[r] > 3
        c2, c3 = cols[r, 2], cols[r, 3]
        v2, v3 = vals_v[r * 4 + 2], vals_v[r * 4 + 3]
        for e in range(6):
            o = e - q - REACH
            if o == 0:
                block = vals_v[r * 4]
            elif o == by:
                block = vals_v[r * 4 + 1]
            elif -REACH <= o <= REACH:
                name = (row0 + r + o + total_blocks) % total_blocks
                use2 = jnp.logical_and(third, c2 == name).astype(F32).astype(BF16)
                use3 = jnp.logical_and(fourth, c3 == name).astype(F32).astype(BF16)
                block = v2 * use2 + v3 * use3
            else:
                block = jnp.zeros((BLK, BLK), BF16)
            band[h, rows, e * BLK : (e + 1) * BLK] = block

    hid[0:256, :] = dot(band[0, :, 256:768], ext[256:768, :])
    hid[256:512, :] = dot(band[1, :, 0:512], ext[256:768, :])
    loads[2].wait()
    loads[3].wait()

    def forward(h):
        rows = pl.ds(pl.multiple_of(256 * h, 256), 256)
        rim_cols = pl.ds(pl.multiple_of(512 * h, 512), 256)
        halo_rows = pl.ds(pl.multiple_of(768 * h, 256), 256)
        hidden = (hid[rows, :] + dot(band[h, :, rim_cols], ext[halo_rows, :])).astype(BF16)
        hid_t[...] = hidden.T
        preact = dot(hidden, w_v[...])
        sig = 1.0 / (1.0 + jnp.exp(-preact))
        out[rows, :] = (preact * sig).astype(BF16)
        slope = sig * (1.0 + preact * (1.0 - sig))
        grad_pre[rows, :] = (cot_v[rows, :].astype(F32) * slope).astype(BF16)

    def rim(h):
        return pltpu.make_async_remote_copy(
            src_ref=rim_out.at[h], dst_ref=rim_in.at[1 - h],
            send_sem=rim_send.at[h], recv_sem=rim_recv.at[1 - h],
            device_id=at_index((me + count - 1 + 2 * h) % count), device_id_type=MESH,
        )

    def send_rim(h):
        rows = pl.ds(pl.multiple_of(256 * h, 256), 256)
        rim_cols = pl.ds(pl.multiple_of(512 * h, 512), 256)
        grad_hid[rows, :] = dot(grad_pre[rows, :], w_v[...], ((1,), (1,))).astype(BF16)
        rim_out[h] = dot(band[h, :, rim_cols], grad_hid[rows, :], ((0,), (0,))).astype(BF16)
        rim(h).start()

    def backward(h, first):
        rows = pl.ds(pl.multiple_of(256 * h, 256), 256)
        inner_cols = pl.ds(pl.multiple_of(256 * (1 - h), 256), 512)
        inner = dot(band[h, :, inner_cols], grad_hid[rows, :], ((0,), (0,)))
        if first:
            gf[...] = inner
        else:
            gf[...] += inner

    pltpu.make_async_remote_copy(
        src_ref=ext.at[pl.ds(256, 256)], dst_ref=ext.at[pl.ds(pl.multiple_of(768 * near, 256), 256)],
        send_sem=halo_send.at[0], recv_sem=halo_recv.at[near],
        device_id=partner, device_id_type=MESH,
    ).wait_recv()
    forward(near)
    acc[...] = dot(hid_t[...], grad_pre[pl.ds(pl.multiple_of(256 * near, 256), 256), :])
    send_rim(near)
    pltpu.make_async_remote_copy(
        src_ref=ext.at[pl.ds(256, 256)], dst_ref=ext.at[pl.ds(pl.multiple_of(768 * far, 256), 256)],
        send_sem=halo_send.at[0], recv_sem=halo_recv.at[far],
        device_id=partner, device_id_type=MESH,
    ).wait_recv()
    forward(far)
    send_rim(far)

    far_rows = pl.ds(pl.multiple_of(256 * far, 256), 256)
    size = 256 // PIECES
    core_copies = []
    for q in range(PIECES):
        here = pl.ds(pl.multiple_of(256 * (1 - core) + size * q, size), size)
        core_out[q] = (acc[here, :] + dot(hid_t[here, :], grad_pre[far_rows, :])).astype(BF16)
        copy = pltpu.make_async_remote_copy(
            src_ref=core_out.at[q], dst_ref=core_in.at[q],
            send_sem=core_send.at[q], recv_sem=core_recv.at[q],
            device_id=partner, device_id_type=MESH,
        )
        copy.start()
        core_copies.append(copy)
    mine = pl.ds(pl.multiple_of(256 * core, 256), 256)
    own_half[...] = acc[mine, :] + dot(hid_t[mine, :], grad_pre[far_rows, :])

    width = 256 // n
    low = width // 2
    for q in range(PIECES):
        core_copies[q].wait_recv()
        chip = (own_half[size * q : size * (q + 1), :] + core_in[q].astype(F32)).astype(BF16)
        for i in range(n // PIECES):
            k = q * (n // PIECES) + i
            sa[k] = chip[width * i : width * i + low, 0:384]
            sb[k] = chip[width * i + low : width * (i + 1), 0:384]
            sc[k] = chip[width * i : width * (i + 1), 384:512]

    parts = ((sa, ra, ta, ua, fa), (sb, rb, tb, ub, fb), (sc, rc, tc, uc, fc))

    def send(src, dst, part, step, axis, value):
        pltpu.make_async_remote_copy(
            src_ref=src, dst_ref=dst, send_sem=step_send.at[part, step], recv_sem=step_recv.at[part, step],
            device_id=peer(axis, value), device_id_type=MESH,
        ).start()

    def arrived(buf, part, step):
        whole = buf.at[pl.ds(0, n - 1)]
        pltpu.make_async_remote_copy(
            src_ref=whole, dst_ref=whole, send_sem=step_send.at[part, step], recv_sem=step_recv.at[part, step],
            device_id=partner, device_id_type=MESH,
        ).wait_recv()

    def summed(buf):
        total = buf[0].astype(F32)
        for i in range(1, n):
            total = total + buf[i].astype(F32)
        return total.astype(BF16)

    pl.semaphore_wait(ready, len(beside))
    for d in hops:
        for p, (s, r, t, u, f) in enumerate(parts):
            axis = ORDERS[p][0]
            j = (place[axis] + d) % n
            send(s.at[j], r.at[place[axis]], p, 0, axis, j)
    for p, (s, r, t, u, f) in enumerate(parts):
        i = place[ORDERS[p][0]]
        r[i] = s[i]
    backward(far, True)

    def spread(p, part, step, distances):
        axis = ORDERS[p][step]
        here = part[step + 1].at[place[axis]]
        for d in distances:
            send(here, here, p, step, axis, (place[axis] + d) % n)

    for step in (1, 2):
        for p, part in enumerate(parts):
            axis = ORDERS[p][step]
            arrived(part[step], p, step - 1)
            part[step + 1][place[axis]] = summed(part[step])
            spread(p, part, step, hops[:FAR])
        for p, part in enumerate(parts):
            spread(p, part, step, hops[FAR:])
        if step == 1:
            backward(near, False)
        else:
            for h in range(2):
                pltpu.make_async_remote_copy(
                    src_ref=rim_out.at[h], dst_ref=rim_in.at[h],
                    send_sem=rim_send.at[h], recv_sem=rim_recv.at[h],
                    device_id=partner, device_id_type=MESH,
                ).wait_recv()
                gf[256 * h : 256 * (h + 1), :] += rim_in[h].astype(F32)

    def gather(p, f, target, slot):
        here = f.at[core, slot]
        axis = ORDERS[p][0]
        return pltpu.make_async_remote_copy(
            src_ref=here, dst_ref=here, send_sem=gather_send.at[p], recv_sem=gather_recv.at[p, slot],
            device_id=peer(axis, target), device_id_type=MESH,
        )

    def onward(p, f, slot):
        here = f.at[core, slot]
        return pltpu.make_async_remote_copy(
            src_ref=here, dst_ref=here, send_sem=fwd_send.at[p], recv_sem=fwd_recv.at[p],
            device_id=partner, device_id_type=MESH,
        )

    for p, part in enumerate(parts):
        i = place[ORDERS[p][0]]
        arrived(part[3], p, 2)
        part[4][core, i] = summed(part[3])
        for d in hops[:FAR]:
            gather(p, part[4], (i + d) % n, i).start()
    for p, part in enumerate(parts):
        i = place[ORDERS[p][0]]
        for d in hops[FAR:]:
            gather(p, part[4], (i + d) % n, i).start()
    for p, part in enumerate(parts):
        onward(p, part[4], place[ORDERS[p][0]]).start()
    for d in hops[::-1]:
        for p, part in enumerate(parts):
            i = place[ORDERS[p][0]]
            j = (i + d) % n
            gather(p, part[4], j, j).wait_recv()
            onward(p, part[4], j).start()

    for h in range(2):
        halo(h).wait_send()
        pltpu.make_async_remote_copy(
            src_ref=rim_out.at[h], dst_ref=rim_in.at[h],
            send_sem=rim_send.at[h], recv_sem=rim_recv.at[h],
            device_id=partner, device_id_type=MESH,
        ).wait_send()
    for copy in core_copies:
        copy.wait_send()
    for p, part in enumerate(parts):
        for step in range(3):
            whole = part[0].at[pl.ds(0, n - 1)]
            pltpu.make_async_remote_copy(
                src_ref=whole, dst_ref=whole, send_sem=step_send.at[p, step], recv_sem=step_recv.at[p, step],
                device_id=partner, device_id_type=MESH,
            ).wait_send()
        whole = part[4].at[core, pl.ds(0, n - 1)]
        pltpu.make_async_remote_copy(
            src_ref=whole, dst_ref=whole, send_sem=gather_send.at[p], recv_sem=fwd_recv.at[p],
            device_id=partner, device_id_type=MESH,
        ).wait_send()
        for_partner = part[4].at[core]
        from_partner = part[4].at[1 - core]
        pltpu.make_async_remote_copy(
            src_ref=for_partner, dst_ref=from_partner, send_sem=fwd_send.at[p], recv_sem=fwd_recv.at[p],
            device_id=partner, device_id_type=MESH,
        ).wait()


def write_kernel(n, out, gf, fa, fb, fc, out_r, gf_r, gw_r, gw, sems):
    copies = [
        pltpu.make_async_copy(out, out_r, sems.at[0]),
        pltpu.make_async_copy(gf, gf_r, sems.at[1]),
    ]
    for copy in copies:
        copy.start()
    width = 256 // n
    low = width // 2
    for c in range(2):
        for k in range(n):
            top = 256 * c + width * k
            gw[top : top + low, 0:384] = fa[c, k].astype(F32)
            gw[top + low : top + width, 0:384] = fb[c, k].astype(F32)
            gw[top : top + width, 384:512] = fc[c, k].astype(F32)
        rows = pl.ds(256 * c, 256)
        copy = pltpu.make_async_copy(gw.at[rows], gw_r.at[rows], sems.at[2 + c])
        copy.start()
        copies.append(copy)
    for copy in copies:
        copy.wait()


def per_device(n, features, adj_cols, adj_counts, adj_vals, weight, cotangent):
    width = 256 // n
    low = width // 2
    vmem = pl.BlockSpec(memory_space=pltpu.VMEM)
    smem = pl.BlockSpec(memory_space=pltpu.SMEM)
    anyw = pl.BlockSpec(memory_space=pl.ANY)
    hbm = pl.BlockSpec(memory_space=pltpu.HBM)
    shapes = ((n, low, 384), (n, low, 384), (n, width, 128))
    dma = pltpu.SemaphoreType.DMA
    steps = [pltpu.VMEM(s, BF16) for _ in range(4) for s in shapes]
    args = (
        adj_cols,
        adj_counts,
        features.reshape(512, 512),
        adj_vals.reshape(16, BLK, BLK),
        weight,
        cotangent.reshape(512, 512),
    )
    out, gf, fa, fb, fc = pl.pallas_call(
        functools.partial(main_kernel, n, 4 * 2 * n**3),
        out_shape=(
            pltpu.VMEM((512, 512), BF16),
            pltpu.VMEM((512, 512), F32),
            *[pltpu.VMEM((2,) + s, BF16) for s in shapes],
        ),
        in_specs=[hbm] * 6,
        out_specs=(vmem,) * 5,
        scratch_shapes=[
            pltpu.SMEM((4, 4), jnp.int32),
            pltpu.SMEM((4,), jnp.int32),
            pltpu.VMEM((1024, 512), BF16),
            pltpu.VMEM((16, BLK, BLK), BF16),
            pltpu.VMEM((512, 512), BF16),
            pltpu.VMEM((512, 512), BF16),
            pltpu.VMEM((2, 256, 768), BF16),
            pltpu.VMEM((512, 512), F32),
            pltpu.VMEM((512, 512), BF16),
            pltpu.VMEM((512, 512), BF16),
            pltpu.VMEM((512, 256), BF16),
            pltpu.VMEM((512, 512), F32),
            pltpu.VMEM((256, 512), F32),
            pltpu.VMEM((PIECES, 256 // PIECES, 512), BF16),
            pltpu.VMEM((PIECES, 256 // PIECES, 512), BF16),
            pltpu.VMEM((2, 256, 512), BF16),
            pltpu.VMEM((2, 256, 512), BF16),
            *steps,
            pltpu.SemaphoreType.REGULAR, dma((6,)), dma((2,)), dma((2,)), dma((2,)), dma((2,)), dma((PIECES,)), dma((PIECES,)),
            dma((3, 3)), dma((3, 3)), dma((3,)), dma((3, n)), dma((3,)), dma((3,)),
        ],
        compiler_params=pltpu.CompilerParams(
            collective_id=0, has_side_effects=True, vmem_limit_bytes=40 * 2**20
        ),
        name="layer",
    )(*[pltpu.with_memory_space_constraint(a, pltpu.HBM) for a in args])
    out, gf, gw = pl.pallas_call(
        functools.partial(write_kernel, n),
        out_shape=(
            jax.ShapeDtypeStruct((512, 512), BF16),
            jax.ShapeDtypeStruct((512, 512), F32),
            jax.ShapeDtypeStruct((512, 512), F32),
        ),
        in_specs=[vmem] * 5,
        out_specs=(anyw,) * 3,
        scratch_shapes=[pltpu.VMEM((512, 512), F32), dma((4,))],
        compiler_params=pltpu.CompilerParams(vmem_limit_bytes=16 * 2**20),
        name="write",
    )(out, gf, fa, fb, fc)
    return out.reshape(4, BLK, 512), gf.reshape(4, BLK, 512), gw


def solution(mesh):
    n = mesh.shape["rep"] // 2
    both = ("own", "rep")
    return jax.shard_map(
        functools.partial(per_device, n),
        mesh=mesh,
        in_specs=(
            P(both, None, None),
            P(both, None),
            P(both),
            P(both, None, None, None),
            P(),
            P(both, None, None),
        ),
        out_specs=(P(both, None, None), P(both, None, None), P()),
        check_vma=False,
    )
```

```python
import functools

import jax
import jax.numpy as jnp
from jax import lax
from jax.experimental import pallas as pl
from jax.experimental.pallas import tpu as pltpu
from jax.sharding import PartitionSpec as P

MESH = pl.DeviceIdType.MESH
F32 = jnp.float32
BF16 = jnp.bfloat16
REACH = 2
BLK = 128
PIECES = 2
FAR = 3
ORDERS = ((1, 0, 2), (0, 2, 1), (2, 1, 0))


def dot(a, b, dims=((1,), (0,))):
    return lax.dot_general(a, b, (dims, ((), ())), preferred_element_type=F32)


def main_kernel(
    n, total_blocks,
    cols_h, counts_h, feat, vals, wgt, cot,
    out, gf, fa, fb, fc,
    cols, counts, ext, vals_v, w_v, cot_v, band, hid, grad_hid, grad_pre, hid_t, acc, own_half,
    core_out, core_in, rim_out, rim_in,
    sa, sb, sc, ra, rb, rc, ta, tb, tc, ua, ub, uc,
    ready, load_sem, halo_send, halo_recv, rim_send, rim_recv, core_send, core_recv,
    step_send, step_recv, gather_send, gather_recv, fwd_send, fwd_recv,
):
    own = lax.axis_index("own")
    rep = lax.axis_index("rep")
    core = rep % 2
    place = (own // n, own % n, rep // 2)
    me = own * (2 * n) + rep
    count = n * n * n * 2

    def device(z, x, y, c):
        return {"own": z * n + x, "rep": y * 2 + c}

    def peer(axis, value):
        p = list(place)
        p[axis] = value
        return device(*p, core)

    def at_index(i):
        return {"own": i // (2 * n), "rep": i % (2 * n)}

    right = at_index((me + 1) % count)
    left = at_index((me + count - 1) % count)
    partner = device(*place, 1 - core)
    hops = sorted(range(1, n), key=lambda d: -min(d, n - d))

    loads = [
        pltpu.make_async_copy(feat, ext.at[pl.ds(256, 512)], load_sem.at[0]),
        pltpu.make_async_copy(vals, vals_v, load_sem.at[1]),
        pltpu.make_async_copy(wgt, w_v, load_sem.at[2]),
        pltpu.make_async_copy(cot, cot_v, load_sem.at[3]),
        pltpu.make_async_copy(cols_h, cols, load_sem.at[4]),
        pltpu.make_async_copy(counts_h, counts, load_sem.at[5]),
    ]
    barrier = pltpu.get_barrier_semaphore()
    for neighbour in (left, right):
        pl.semaphore_signal(barrier, inc=1, device_id=neighbour, device_id_type=MESH)
    for copy in loads:
        copy.start()
    beside = [(axis, d) for d in sorted({1, n - 1}) for axis in range(3)]
    second = [(axis, d) for d in sorted({d for d in (2, n - 2) if 0 < d < n}) for axis in range(3)]
    for axis, d in beside:
        pl.semaphore_signal(
            barrier, inc=1, device_id=peer(axis, (place[axis] + d) % n), device_id_type=MESH
        )

    loads[0].wait()
    pl.semaphore_wait(barrier, len(beside) + 2)
    def halo(h):
        return pltpu.make_async_remote_copy(
            src_ref=ext.at[pl.ds(pl.multiple_of(256 + 256 * h, 256), 256)],
            dst_ref=ext.at[pl.ds(pl.multiple_of(768 * (1 - h), 256), 256)],
            send_sem=halo_send.at[h], recv_sem=halo_recv.at[1 - h],
            device_id=at_index((me + count - 1 + 2 * h) % count), device_id_type=MESH,
        )

    near, far = 1 - core, core
    halo(far).start()
    halo(near).start()
    for axis, d in beside:
        pl.semaphore_signal(
            ready.at[0], inc=1, device_id=peer(axis, (place[axis] + d) % n), device_id_type=MESH
        )

    row0 = me * 4
    loads[4].wait()
    loads[5].wait()
    loads[1].wait()
    for r in range(4):
        h, q = divmod(r, 2)
        rows = slice(q * BLK, (q + 1) * BLK)
        by = -1 if q == 0 else 1
        third = counts[r] > 2
        fourth = counts[r] > 3
        c2, c3 = cols[r, 2], cols[r, 3]
        v2, v3 = vals_v[r * 4 + 2], vals_v[r * 4 + 3]
        for e in range(6):
            o = e - q - REACH
            if o == 0:
                block = vals_v[r * 4]
            elif o == by:
                block = vals_v[r * 4 + 1]
            elif -REACH <= o <= REACH:
                name = (row0 + r + o + total_blocks) % total_blocks
                use2 = jnp.logical_and(third, c2 == name).astype(F32).astype(BF16)
                use3 = jnp.logical_and(fourth, c3 == name).astype(F32).astype(BF16)
                block = v2 * use2 + v3 * use3
            else:
                block = jnp.zeros((BLK, BLK), BF16)
            band[h, rows, e * BLK : (e + 1) * BLK] = block

    hid[0:256, :] = dot(band[0, :, 256:768], ext[256:768, :])
    hid[256:512, :] = dot(band[1, :, 0:512], ext[256:768, :])
    loads[2].wait()
    loads[3].wait()

    def forward(h):
        rows = pl.ds(pl.multiple_of(256 * h, 256), 256)
        rim_cols = pl.ds(pl.multiple_of(512 * h, 512), 256)
        halo_rows = pl.ds(pl.multiple_of(768 * h, 256), 256)
        hidden = (hid[rows, :] + dot(band[h, :, rim_cols], ext[halo_rows, :])).astype(BF16)
        hid_t[...] = hidden.T
        preact = dot(hidden, w_v[...])
        sig = 1.0 / (1.0 + jnp.exp(-preact))
        out[rows, :] = (preact * sig).astype(BF16)
        slope = sig * (1.0 + preact * (1.0 - sig))
        grad_pre[rows, :] = (cot_v[rows, :].astype(F32) * slope).astype(BF16)

    def rim(h):
        return pltpu.make_async_remote_copy(
            src_ref=rim_out.at[h], dst_ref=rim_in.at[1 - h],
            send_sem=rim_send.at[h], recv_sem=rim_recv.at[1 - h],
            device_id=at_index((me + count - 1 + 2 * h) % count), device_id_type=MESH,
        )

    def send_rim(h):
        rows = pl.ds(pl.multiple_of(256 * h, 256), 256)
        rim_cols = pl.ds(pl.multiple_of(512 * h, 512), 256)
        grad_hid[rows, :] = dot(grad_pre[rows, :], w_v[...], ((1,), (1,))).astype(BF16)
        rim_out[h] = dot(band[h, :, rim_cols], grad_hid[rows, :], ((0,), (0,))).astype(BF16)
        rim(h).start()

    def backward(h, first):
        rows = pl.ds(pl.multiple_of(256 * h, 256), 256)
        inner_cols = pl.ds(pl.multiple_of(256 * (1 - h), 256), 512)
        inner = dot(band[h, :, inner_cols], grad_hid[rows, :], ((0,), (0,)))
        if first:
            gf[...] = inner
        else:
            gf[...] += inner

    pltpu.make_async_remote_copy(
        src_ref=ext.at[pl.ds(256, 256)], dst_ref=ext.at[pl.ds(pl.multiple_of(768 * near, 256), 256)],
        send_sem=halo_send.at[0], recv_sem=halo_recv.at[near],
        device_id=partner, device_id_type=MESH,
    ).wait_recv()
    forward(near)
    acc[...] = dot(hid_t[...], grad_pre[pl.ds(pl.multiple_of(256 * near, 256), 256), :])
    send_rim(near)
    pl.semaphore_wait(ready.at[0], len(beside))
    for axis, d in second:
        pl.semaphore_signal(
            ready.at[1], inc=1, device_id=peer(axis, (place[axis] + d) % n), device_id_type=MESH
        )
    pltpu.make_async_remote_copy(
        src_ref=ext.at[pl.ds(256, 256)], dst_ref=ext.at[pl.ds(pl.multiple_of(768 * far, 256), 256)],
        send_sem=halo_send.at[0], recv_sem=halo_recv.at[far],
        device_id=partner, device_id_type=MESH,
    ).wait_recv()
    forward(far)
    send_rim(far)

    far_rows = pl.ds(pl.multiple_of(256 * far, 256), 256)
    size = 256 // PIECES
    core_copies = []
    for q in range(PIECES):
        here = pl.ds(pl.multiple_of(256 * (1 - core) + size * q, size), size)
        core_out[q] = (acc[here, :] + dot(hid_t[here, :], grad_pre[far_rows, :])).astype(BF16)
        copy = pltpu.make_async_remote_copy(
            src_ref=core_out.at[q], dst_ref=core_in.at[q],
            send_sem=core_send.at[q], recv_sem=core_recv.at[q],
            device_id=partner, device_id_type=MESH,
        )
        copy.start()
        core_copies.append(copy)
    mine = pl.ds(pl.multiple_of(256 * core, 256), 256)
    own_half[...] = acc[mine, :] + dot(hid_t[mine, :], grad_pre[far_rows, :])

    width = 256 // n
    low = width // 2
    for q in range(PIECES):
        core_copies[q].wait_recv()
        chip = (own_half[size * q : size * (q + 1), :] + core_in[q].astype(F32)).astype(BF16)
        for i in range(n // PIECES):
            k = q * (n // PIECES) + i
            sa[k] = chip[width * i : width * i + low, 0:384]
            sb[k] = chip[width * i + low : width * (i + 1), 0:384]
            sc[k] = chip[width * i : width * (i + 1), 384:512]

    parts = ((sa, ra, ta, ua, fa), (sb, rb, tb, ub, fb), (sc, rc, tc, uc, fc))

    def send(src, dst, part, step, axis, value):
        pltpu.make_async_remote_copy(
            src_ref=src, dst_ref=dst, send_sem=step_send.at[part, step], recv_sem=step_recv.at[part, step],
            device_id=peer(axis, value), device_id_type=MESH,
        ).start()

    def arrived(buf, part, step):
        whole = buf.at[pl.ds(0, n - 1)]
        pltpu.make_async_remote_copy(
            src_ref=whole, dst_ref=whole, send_sem=step_send.at[part, step], recv_sem=step_recv.at[part, step],
            device_id=partner, device_id_type=MESH,
        ).wait_recv()

    def summed(buf):
        total = buf[0].astype(F32)
        for i in range(1, n):
            total = total + buf[i].astype(F32)
        return total.astype(BF16)

    if second:
        pl.semaphore_wait(ready.at[1], len(second))
    for d in hops:
        for p, (s, r, t, u, f) in enumerate(parts):
            axis = ORDERS[p][0]
            j = (place[axis] + d) % n
            send(s.at[j], r.at[place[axis]], p, 0, axis, j)
    for p, (s, r, t, u, f) in enumerate(parts):
        i = place[ORDERS[p][0]]
        r[i] = s[i]
    backward(far, True)

    def spread(p, part, step, distances):
        axis = ORDERS[p][step]
        here = part[step + 1].at[place[axis]]
        for d in distances:
            send(here, here, p, step, axis, (place[axis] + d) % n)

    for step in (1, 2):
        for p, part in enumerate(parts):
            axis = ORDERS[p][step]
            arrived(part[step], p, step - 1)
            part[step + 1][place[axis]] = summed(part[step])
            spread(p, part, step, hops[:FAR])
        for p, part in enumerate(parts):
            spread(p, part, step, hops[FAR:])
        if step == 1:
            backward(near, False)
        else:
            for h in range(2):
                pltpu.make_async_remote_copy(
                    src_ref=rim_out.at[h], dst_ref=rim_in.at[h],
                    send_sem=rim_send.at[h], recv_sem=rim_recv.at[h],
                    device_id=partner, device_id_type=MESH,
                ).wait_recv()
                gf[256 * h : 256 * (h + 1), :] += rim_in[h].astype(F32)

    def gather(p, f, target, slot):
        here = f.at[core, slot]
        axis = ORDERS[p][0]
        return pltpu.make_async_remote_copy(
            src_ref=here, dst_ref=here, send_sem=gather_send.at[p], recv_sem=gather_recv.at[p, slot],
            device_id=peer(axis, target), device_id_type=MESH,
        )

    def onward(p, f, slot):
        here = f.at[core, slot]
        return pltpu.make_async_remote_copy(
            src_ref=here, dst_ref=here, send_sem=fwd_send.at[p], recv_sem=fwd_recv.at[p],
            device_id=partner, device_id_type=MESH,
        )

    for p, part in enumerate(parts):
        i = place[ORDERS[p][0]]
        arrived(part[3], p, 2)
        part[4][core, i] = summed(part[3])
        for d in hops[:FAR]:
            gather(p, part[4], (i + d) % n, i).start()
    for p, part in enumerate(parts):
        i = place[ORDERS[p][0]]
        for d in hops[FAR:]:
            gather(p, part[4], (i + d) % n, i).start()
    for p, part in enumerate(parts):
        onward(p, part[4], place[ORDERS[p][0]]).start()
    for d in hops[::-1]:
        for p, part in enumerate(parts):
            i = place[ORDERS[p][0]]
            j = (i + d) % n
            gather(p, part[4], j, j).wait_recv()
            onward(p, part[4], j).start()

    for h in range(2):
        halo(h).wait_send()
        pltpu.make_async_remote_copy(
            src_ref=rim_out.at[h], dst_ref=rim_in.at[h],
            send_sem=rim_send.at[h], recv_sem=rim_recv.at[h],
            device_id=partner, device_id_type=MESH,
        ).wait_send()
    for copy in core_copies:
        copy.wait_send()
    for p, part in enumerate(parts):
        for step in range(3):
            whole = part[0].at[pl.ds(0, n - 1)]
            pltpu.make_async_remote_copy(
                src_ref=whole, dst_ref=whole, send_sem=step_send.at[p, step], recv_sem=step_recv.at[p, step],
                device_id=partner, device_id_type=MESH,
            ).wait_send()
        whole = part[4].at[core, pl.ds(0, n - 1)]
        pltpu.make_async_remote_copy(
            src_ref=whole, dst_ref=whole, send_sem=gather_send.at[p], recv_sem=fwd_recv.at[p],
            device_id=partner, device_id_type=MESH,
        ).wait_send()
        for_partner = part[4].at[core]
        from_partner = part[4].at[1 - core]
        pltpu.make_async_remote_copy(
            src_ref=for_partner, dst_ref=from_partner, send_sem=fwd_send.at[p], recv_sem=fwd_recv.at[p],
            device_id=partner, device_id_type=MESH,
        ).wait()


def write_kernel(n, out, gf, fa, fb, fc, out_r, gf_r, gw_r, gw, sems):
    copies = [
        pltpu.make_async_copy(out, out_r, sems.at[0]),
        pltpu.make_async_copy(gf, gf_r, sems.at[1]),
    ]
    for copy in copies:
        copy.start()
    width = 256 // n
    low = width // 2
    for c in range(2):
        for k in range(n):
            top = 256 * c + width * k
            gw[top : top + low, 0:384] = fa[c, k].astype(F32)
            gw[top + low : top + width, 0:384] = fb[c, k].astype(F32)
            gw[top : top + width, 384:512] = fc[c, k].astype(F32)
        rows = pl.ds(256 * c, 256)
        copy = pltpu.make_async_copy(gw.at[rows], gw_r.at[rows], sems.at[2 + c])
        copy.start()
        copies.append(copy)
    for copy in copies:
        copy.wait()


def per_device(n, features, adj_cols, adj_counts, adj_vals, weight, cotangent):
    width = 256 // n
    low = width // 2
    vmem = pl.BlockSpec(memory_space=pltpu.VMEM)
    smem = pl.BlockSpec(memory_space=pltpu.SMEM)
    anyw = pl.BlockSpec(memory_space=pl.ANY)
    hbm = pl.BlockSpec(memory_space=pltpu.HBM)
    shapes = ((n, low, 384), (n, low, 384), (n, width, 128))
    dma = pltpu.SemaphoreType.DMA
    steps = [pltpu.VMEM(s, BF16) for _ in range(4) for s in shapes]
    args = (
        adj_cols,
        adj_counts,
        features.reshape(512, 512),
        adj_vals.reshape(16, BLK, BLK),
        weight,
        cotangent.reshape(512, 512),
    )
    out, gf, fa, fb, fc = pl.pallas_call(
        functools.partial(main_kernel, n, 4 * 2 * n**3),
        out_shape=(
            pltpu.VMEM((512, 512), BF16),
            pltpu.VMEM((512, 512), F32),
            *[pltpu.VMEM((2,) + s, BF16) for s in shapes],
        ),
        in_specs=[hbm] * 6,
        out_specs=(vmem,) * 5,
        scratch_shapes=[
            pltpu.SMEM((4, 4), jnp.int32),
            pltpu.SMEM((4,), jnp.int32),
            pltpu.VMEM((1024, 512), BF16),
            pltpu.VMEM((16, BLK, BLK), BF16),
            pltpu.VMEM((512, 512), BF16),
            pltpu.VMEM((512, 512), BF16),
            pltpu.VMEM((2, 256, 768), BF16),
            pltpu.VMEM((512, 512), F32),
            pltpu.VMEM((512, 512), BF16),
            pltpu.VMEM((512, 512), BF16),
            pltpu.VMEM((512, 256), BF16),
            pltpu.VMEM((512, 512), F32),
            pltpu.VMEM((256, 512), F32),
            pltpu.VMEM((PIECES, 256 // PIECES, 512), BF16),
            pltpu.VMEM((PIECES, 256 // PIECES, 512), BF16),
            pltpu.VMEM((2, 256, 512), BF16),
            pltpu.VMEM((2, 256, 512), BF16),
            *steps,
            pltpu.SemaphoreType.REGULAR((2,)), dma((6,)), dma((2,)), dma((2,)), dma((2,)), dma((2,)), dma((PIECES,)), dma((PIECES,)),
            dma((3, 3)), dma((3, 3)), dma((3,)), dma((3, n)), dma((3,)), dma((3,)),
        ],
        compiler_params=pltpu.CompilerParams(
            collective_id=0, has_side_effects=True, vmem_limit_bytes=40 * 2**20
        ),
        name="layer",
    )(*[pltpu.with_memory_space_constraint(a, pltpu.HBM) for a in args])
    out, gf, gw = pl.pallas_call(
        functools.partial(write_kernel, n),
        out_shape=(
            jax.ShapeDtypeStruct((512, 512), BF16),
            jax.ShapeDtypeStruct((512, 512), F32),
            jax.ShapeDtypeStruct((512, 512), F32),
        ),
        in_specs=[vmem] * 5,
        out_specs=(anyw,) * 3,
        scratch_shapes=[pltpu.VMEM((512, 512), F32), dma((4,))],
        compiler_params=pltpu.CompilerParams(vmem_limit_bytes=16 * 2**20),
        name="write",
    )(out, gf, fa, fb, fc)
    return out.reshape(4, BLK, 512), gf.reshape(4, BLK, 512), gw


def solution(mesh):
    n = mesh.shape["rep"] // 2
    both = ("own", "rep")
    return jax.shard_map(
        functools.partial(per_device, n),
        mesh=mesh,
        in_specs=(
            P(both, None, None),
            P(both, None),
            P(both),
            P(both, None, None, None),
            P(),
            P(both, None, None),
        ),
        out_specs=(P(both, None, None), P(both, None, None), P()),
        check_vma=False,
    )
```
